32 devices in a mesh: depth: 4 (over z), row: 2 (over core), col: 4 (over y, x).
Axes of the slice: x: 2, y: 2, z: 4, core: 2. Of those that a mesh axis runs over, the one named last changes fastest.
Arguments:
- linv_root: float32 [4096, 4096], P(('depth', 'row'))
- child_factor: float32 [4, 4096, 2048], P('depth', 'col', 'row'), may hold values from -0.125 to 0.125
- child_inverse: float32 [4, 2048, 2048], P('depth', 'col')
- structure: int32 [4, 32], P('depth', 'col'), may hold values 0 or 1
Outputs:
- sigma_root: float32 [4096, 4096], P(('depth', 'row'), 'col')
- sigma_cross: float32 [4, 4096, 2048], P('depth', 'col', 'row')
- sigma_child: float32 [4, 2048, 2048], P('depth', 'col', 'row')
The draws below stay inside these ranges and needn't reach their ends.
All inputs are finite; a program needn't handle non-finite values. No bound on the sum of `structure` on one device may be relied on, other than what follows from the above.
Results may differ from the reference program's by a relative error of at most 0.00015.
Values sent between devices are 32-bit elements; how exact they have to be, the bound alone decides.
A program may use at most 192 MiB of HBM per device.

```python
import jax
import jax.numpy as jnp
from jax import lax

NR = 4096
NJ = 2048
TILE = 128
CHILDREN = 4


def lower_factor(key, shape, off_scale, diag_low, diag_high):
    off_key, diag_key = jax.random.split(key)
    order = shape[-1]
    row_index = jnp.arange(order)[:, None]
    col_index = jnp.arange(order)[None, :]
    off_part = jax.random.normal(off_key, shape, jnp.float32) * (off_scale / order ** 0.5)
    diag_part = jax.random.uniform(diag_key, shape, jnp.float32, diag_low, diag_high)
    return jnp.where(row_index > col_index, off_part, jnp.where(row_index == col_index, diag_part, 0.0))


def draw_linv_root(key, part):
    key = jax.random.fold_in(key, 1)
    return lower_factor(key, (NR, NR), 1.0, 1.0, 2.0)


def draw_child_inverse(key, part):
    key = jax.random.fold_in(key, 2)
    return lower_factor(key, (CHILDREN, NJ, NJ), 1.0, 1.0, 2.0)


def place_ends(array, own_key, low, high):
    longest = array.shape.index(max(array.shape))
    spots = []
    for shift in (0, 1):
        where = [jax.random.randint(jax.random.fold_in(own_key, axis), (), 0, length) for axis, length in enumerate(array.shape)]
        where[longest] = (where[longest] + shift) % array.shape[longest]
        spots.append(tuple(where))
    return array.at[spots[0]].set(low).at[spots[1]].set(high)


def shard_levels(own_key, shape, cuts, low, top_value):
    gain, own = 1.0, jax.random.fold_in(own_key, 6)
    for position, shards_of in cuts:
        draws = jnp.exp(jax.random.uniform(jax.random.fold_in(own, position), (shards_of,), jnp.float32, low / len(cuts), top_value / len(cuts)))
        gain = gain * jnp.repeat(draws, shape[position] // shards_of).reshape([-1 if axis == position else 1 for axis in range(len(shape))])
    return gain


def noise(own_key, extent, width, limit, pieces=(), kind=jnp.bfloat16):
    result = jax.random.normal(own_key, extent, jnp.float32) * width
    if len(pieces) > 0:
        result = shard_levels(own_key, extent, pieces, -0.22, 0.18) * result
    return jnp.clip(result, min=-limit, max=limit).astype(kind)


def setup_inputs(seed: int = 0) -> dict:
    seeds = jax.random.split(jax.random.key(seed), 5)
    linv_root = draw_linv_root(jax.random.fold_in(seeds[4], 71), 0)
    child_factor = noise(seeds[1], (CHILDREN, NR, NJ), (0.5 / NR ** 0.5), 0.125, ((0, 4), (1, 4), (2, 2)), jnp.float32)
    child_inverse = draw_child_inverse(jax.random.fold_in(seeds[4], 71), 0)
    structure = place_ends((jax.random.randint(seeds[3], (CHILDREN, NR // TILE), 0, 2) < 1).astype(jnp.int32), jax.random.fold_in(seeds[3], 1), 0, 1)
    return {"linv_root": linv_root, "child_factor": child_factor, "child_inverse": child_inverse, "structure": structure}


def reference(linv_root, child_factor, child_inverse, structure):
    highest = lax.Precision.HIGHEST
    sigma_root = jnp.dot(linv_root.T, linv_root, precision=highest, preferred_element_type=jnp.float32)
    row_masks = jnp.repeat(structure, TILE, axis=1).astype(jnp.float32)

    def one_child(items):
        factor, inverse, row_mask = items
        masked_factor = factor * row_mask[:, None]
        update = jnp.dot(masked_factor, inverse, precision=highest, preferred_element_type=jnp.float32)
        weighted = jnp.dot(sigma_root, update, precision=highest, preferred_element_type=jnp.float32)
        cross_block = -weighted * row_mask[:, None]
        child_block = jnp.dot(inverse.T, inverse, precision=highest, preferred_element_type=jnp.float32)
        child_block = child_block + jnp.dot(update.T, weighted, precision=highest, preferred_element_type=jnp.float32)
        return cross_block, child_block

    sigma_cross, sigma_child = lax.map(one_child, (child_factor, child_inverse, row_masks))
    return sigma_root, sigma_cross, sigma_child
```

```python
import jax
import jax.numpy as jnp
from jax import lax
from jax.experimental import pallas as pl
from jax.experimental.pallas import tpu as pltpu
from jax.sharding import PartitionSpec as P

TILE = 128
PIECES = 4
CHILD_PARTS = 2
PRECISION = lax.Precision.HIGH
MESH = pl.DeviceIdType.MESH


def contract_rows(left, right):
    return lax.dot_general(
        left,
        right,
        (((0,), (0,)), ((), ())),
        precision=PRECISION,
        preferred_element_type=jnp.float32,
    )


def product(left, right):
    return jnp.dot(left, right, precision=PRECISION, preferred_element_type=jnp.float32)


def places():
    return lax.axis_index("depth"), lax.axis_index("row"), lax.axis_index("col")


def across(col_at):
    return col_at + 1 - 2 * lax.rem(col_at, 2), lax.rem(col_at + 2, 4), 3 - col_at


def enter(depth_at, row_at, col_at, n_depth):
    barrier = pltpu.get_barrier_semaphore()
    by_x, by_y, _ = across(col_at)
    for device in ({"row": 1 - row_at}, {"col": by_x}, {"col": by_y}):
        pl.semaphore_signal(barrier, inc=1, device_id=device, device_id_type=MESH)

    @pl.when(depth_at > 0)
    def _():
        pl.semaphore_signal(barrier, inc=1, device_id={"depth": depth_at - 1}, device_id_type=MESH)

    @pl.when(depth_at < n_depth - 1)
    def _():
        pl.semaphore_signal(barrier, inc=1, device_id={"depth": depth_at + 1}, device_id_type=MESH)

    ends = jnp.where(depth_at == 0, 1, 0) + jnp.where(depth_at == n_depth - 1, 1, 0)
    pl.semaphore_wait(barrier, 5 - ends)


def remote(source, target, send, recv, device):
    return pltpu.make_async_remote_copy(
        src_ref=source, dst_ref=target, send_sem=send, recv_sem=recv, device_id=device, device_id_type=MESH
    )


class SquareGather:
    def __init__(self, own, gathered, col_at, send, recv, local):
        half = own.shape[0] // 2
        top, low = pl.ds(0, half), pl.ds(half, half)
        by_x, by_y, far = across(col_at)
        along_x, along_y = {"col": by_x}, {"col": by_y}
        at_x, at_y, at_far = (gathered.at[k] for k in (by_x, by_y, far))
        mine = gathered.at[col_at]
        self.local = pltpu.make_async_copy(own, mine, local)
        self.copies = [
            remote(own.at[low], mine.at[low], send.at[0], recv.at[0], along_x),
            remote(own.at[top], mine.at[top], send.at[1], recv.at[1], along_y),
            remote(own.at[top], mine.at[top], send.at[2], recv.at[2], along_x),
            remote(own.at[low], mine.at[low], send.at[3], recv.at[3], along_y),
            remote(at_y.at[top], at_y.at[top], send.at[4], recv.at[4], along_x),
            remote(at_x.at[low], at_x.at[low], send.at[5], recv.at[5], along_y),
        ]
        arrivals = [at_x.at[low], at_y.at[top], at_x.at[top], at_y.at[low], at_far.at[top], at_far.at[low]]
        self.arrivals = [
            remote(ref, ref, send.at[k], recv.at[k], along_x if k % 2 == 0 else along_y)
            for k, ref in enumerate(arrivals)
        ]

    def first(self):
        self.local.start()
        self.copies[0].start()
        self.copies[1].start()

    def second(self):
        self.arrivals[0].wait_recv()
        self.arrivals[1].wait_recv()
        for copy in self.copies[2:]:
            copy.start()

    def last(self):
        for arrival in self.arrivals[2:]:
            arrival.wait_recv()
        for copy in self.copies:
            copy.wait_send()
        self.local.wait()


def reduce_kernel(
    terms, block, own, gathered, mine, other, rights, lefts,
    core_send, core_recv, local_sem, right_send, right_recv, left_send, left_recv, sq_send, sq_recv, sq_local,
):
    depth_at, row_at, col_at = places()
    n = terms.shape[0]
    rows = terms.shape[2] // PIECES
    enter(depth_at, row_at, col_at, n)
    order = [k for pair in zip(range(n - 1, -1, -1), range(n)) for k in pair][:n]
    core = [
        remote(terms.at[k, 1 - row_at], other.at[k], core_send.at[k], core_recv.at[k], {"row": 1 - row_at})
        for k in range(n)
    ]
    local = [pltpu.make_async_copy(terms.at[k, row_at], mine.at[k], local_sem.at[k]) for k in range(n)]
    for k in order:
        core[k].start()
        local[k].start()
    square = SquareGather(block, gathered, col_at, sq_send, sq_recv, sq_local)
    square.first()
    for k in order:
        core[k].wait_recv()
        local[k].wait()
        mine[k] += other[k]

    def onward(piece, k, going, buffer, send, recv, first, device):
        at = pl.ds(piece * rows, rows)
        here = buffer.at[k, at]
        straight = remote(mine.at[k, at], here, send.at[k, piece], recv.at[k, piece], device)
        summed = remote(here, here, send.at[k, piece], recv.at[k, piece], device)

        @pl.when(first)
        def _():
            straight.start()

        @pl.when(jnp.logical_and(going, jnp.logical_not(first)))
        def _():
            summed.wait_recv()
            buffer[k, at] += mine[k, at]
            summed.start()

    to_right, to_left = {"depth": depth_at + 1}, {"depth": depth_at - 1}
    for piece in range(PIECES):
        at = pl.ds(piece * rows, rows)
        for step in range(n - 1):
            right_k, left_k = n - 1 - step, step
            onward(piece, right_k, depth_at < right_k, rights, right_send, right_recv, depth_at == 0, to_right)
            onward(piece, left_k, depth_at > left_k, lefts, left_send, left_recv, depth_at == n - 1, to_left)
        own[at] = mine[depth_at, at]

        @pl.when(depth_at > 0)
        def _():
            here = rights.at[depth_at, at]
            remote(here, here, right_send.at[depth_at, piece], right_recv.at[depth_at, piece], to_left).wait_recv()
            own[at] += rights[depth_at, at]

        @pl.when(depth_at < n - 1)
        def _():
            here = lefts.at[depth_at, at]
            remote(here, here, left_send.at[depth_at, piece], left_recv.at[depth_at, piece], to_right).wait_recv()
            own[at] += lefts[depth_at, at]

        if piece == 0:
            square.second()
    for piece in range(PIECES):
        at = pl.ds(piece * rows, rows)
        for k in range(n):

            @pl.when(depth_at < k)
            def _():
                remote(mine.at[k, at], rights.at[k, at], right_send.at[k, piece], right_recv.at[k, piece], to_right).wait_send()

            @pl.when(depth_at > k)
            def _():
                remote(mine.at[k, at], lefts.at[k, at], left_send.at[k, piece], left_recv.at[k, piece], to_left).wait_send()

    for k in range(n):
        core[k].wait_send()
    square.last()


def spread_kernel(
    own, block, panel, gathered,
    core_send, core_recv, local_sem, right_send, right_recv, left_send, left_recv, sq_send, sq_recv, sq_local,
):
    depth_at, row_at, col_at = places()
    n = panel.shape[0]
    enter(depth_at, row_at, col_at, n)
    square = SquareGather(block, gathered, col_at, sq_send, sq_recv, sq_local)
    square.first()
    local = pltpu.make_async_copy(own, panel.at[depth_at, row_at], local_sem)
    local.start()
    sibling = {"row": 1 - row_at}
    to_right, to_left = {"depth": depth_at + 1}, {"depth": depth_at - 1}

    def pass_on(source, k, send, recv, device):
        return remote(source, panel.at[k, row_at], send.at[k], recv.at[k], device)

    @pl.when(depth_at < n - 1)
    def _():
        pass_on(own, depth_at, right_send, right_recv, to_right).start()

    @pl.when(depth_at > 0)
    def _():
        pass_on(own, depth_at, left_send, left_recv, to_left).start()

    remote(own, panel.at[depth_at, row_at], core_send.at[depth_at], core_recv.at[depth_at], sibling).start()
    for step in range(1, n):

        @pl.when(depth_at >= step)
        def _():
            k = depth_at - step
            here = panel.at[k, row_at]
            pass_on(here, k, right_send, right_recv, to_left).wait_recv()

            @pl.when(depth_at < n - 1)
            def _():
                pass_on(here, k, right_send, right_recv, to_right).start()

            remote(here, here, core_send.at[k], core_recv.at[k], sibling).start()

        @pl.when(depth_at + step < n)
        def _():
            k = depth_at + step
            here = panel.at[k, row_at]
            pass_on(here, k, left_send, left_recv, to_right).wait_recv()

            @pl.when(depth_at > 0)
            def _():
                pass_on(here, k, left_send, left_recv, to_left).start()

            remote(here, here, core_send.at[k], core_recv.at[k], sibling).start()

        if step == 1:
            square.second()
    for k in range(n):

        @pl.when(jnp.logical_and(k <= depth_at, depth_at < n - 1))
        def _():
            pass_on(own, k, right_send, right_recv, to_right).wait_send()

        @pl.when(jnp.logical_and(k >= depth_at, depth_at > 0))
        def _():
            pass_on(own, k, left_send, left_recv, to_left).wait_send()

        theirs = panel.at[k, 1 - row_at]
        arrival = remote(theirs, theirs, core_send.at[k], core_recv.at[k], sibling)
        arrival.wait_recv()
        arrival.wait_send()
    local.wait()
    square.last()


def hbm():
    return pl.BlockSpec(memory_space=pl.ANY)


def reduce_and_gather(terms, block):
    n, _, rows, width = terms.shape
    dma = pltpu.SemaphoreType.DMA
    landing = pltpu.VMEM((n, rows, width), jnp.float32)
    return pl.pallas_call(
        reduce_kernel,
        out_shape=(
            jax.ShapeDtypeStruct((rows, width), jnp.float32),
            jax.ShapeDtypeStruct((4,) + block.shape, jnp.float32),
        ),
        in_specs=[hbm(), hbm()],
        out_specs=(pl.BlockSpec(memory_space=pltpu.VMEM), hbm()),
        scratch_shapes=[landing] * 4
        + [dma((n,))] * 3
        + [dma((n, PIECES))] * 4
        + [dma((6,)), dma((6,)), dma],
        compiler_params=pltpu.CompilerParams(
            collective_id=1, has_side_effects=True, vmem_limit_bytes=44 * 2**20
        ),
    )(terms, block)


def spread_and_gather(own, block, n):
    dma = pltpu.SemaphoreType.DMA
    return pl.pallas_call(
        spread_kernel,
        out_shape=(
            jax.ShapeDtypeStruct((n, 2) + own.shape, jnp.float32),
            jax.ShapeDtypeStruct((4,) + block.shape, jnp.float32),
        ),
        in_specs=[hbm(), hbm()],
        out_specs=(hbm(), hbm()),
        scratch_shapes=[dma((n,)), dma((n,)), dma] + [dma((n,))] * 4 + [dma((6,)), dma((6,)), dma],
        compiler_params=pltpu.CompilerParams(
            collective_id=2, has_side_effects=True, vmem_limit_bytes=44 * 2**20
        ),
    )(own, block)


def shards(linv_root, child_factor, child_inverse, structure):
    n_col = lax.axis_size("col")
    n_row = lax.axis_size("row")
    n_depth = lax.axis_size("depth")
    depth_at, row_at, col_at = places()
    root_rows = linv_root.shape[0]
    col_width = linv_root.shape[1] // n_col
    root_cols = lax.dynamic_slice_in_dim(linv_root, col_at * col_width, col_width, 1)
    term_value = contract_rows(linv_root, root_cols)
    factor = child_factor[0]
    inverse = child_inverse[0]
    tile_mask = jnp.repeat(structure[0], TILE).astype(jnp.float32)[:, None]
    masked_factor = factor * tile_mask
    factor_panel = lax.all_gather(masked_factor, "row", axis=1, tiled=True)
    nj_row = factor.shape[1]
    inverse_block = lax.dynamic_slice_in_dim(inverse, row_at * nj_row, nj_row, 1)
    if (n_depth, n_row, n_col) == (4, 2, 4):
        terms = term_value.reshape(n_depth, n_row, root_rows, col_width)
        sigma_root, inverse_columns = reduce_and_gather(terms, inverse_block)
        update = product(factor_panel, inverse_columns.reshape(-1, nj_row))
        panel, update_columns = spread_and_gather(sigma_root, update, n_depth)
        column_panel = panel.reshape(-1, col_width)
        update_columns = update_columns.reshape(-1, nj_row)
    else:
        column_panel = lax.psum(term_value, ("depth", "row"))
        flat_at = depth_at * n_row + row_at
        sigma_root = lax.dynamic_slice_in_dim(column_panel, flat_at * root_rows, root_rows, 0)
        update = product(factor_panel, lax.all_gather(inverse_block, "col", axis=0, tiled=True))
        update_columns = lax.all_gather(update, "col", axis=0, tiled=True)
    update_panel = lax.all_gather(update, "row", axis=1, tiled=True)
    weighted = contract_rows(column_panel, update_columns)
    cross_block = -weighted * tile_mask
    part = nj_row // CHILD_PARTS
    child = []
    for k in range(CHILD_PARTS):
        term = contract_rows(update_panel, weighted[:, k * part : (k + 1) * part]) + contract_rows(
            inverse, inverse_block[:, k * part : (k + 1) * part]
        )
        child.append(lax.psum_scatter(term, "col", scatter_dimension=0, tiled=True))
    return (sigma_root, cross_block[None], jnp.concatenate(child, axis=1)[None])


def solution(mesh):
    in_specs = (
        P(("depth", "row"), None),
        P("depth", "col", "row"),
        P("depth", "col", None),
        P("depth", "col"),
    )
    out_specs = (P(("depth", "row"), "col"), P("depth", "col", "row"), P("depth", "col", "row"))
    return jax.shard_map(shards, mesh=mesh, in_specs=in_specs, out_specs=out_specs, check_vma=False)
```

```python
import jax
import jax.numpy as jnp
from jax import lax
from jax.sharding import PartitionSpec as P

TILE = 128
PRECISION = lax.Precision.HIGH


def contract_rows(left, right):
    return lax.dot_general(
        left,
        right,
        (((0,), (0,)), ((), ())),
        precision=PRECISION,
        preferred_element_type=jnp.float32,
    )


def shards(linv_root, child_factor, child_inverse, structure):
    n_col = lax.axis_size("col")
    n_row = lax.axis_size("row")
    col_at = lax.axis_index("col")
    row_at = lax.axis_index("row")
    root_rows = linv_root.shape[0]
    col_width = linv_root.shape[1] // n_col
    flat_at = lax.axis_index("depth") * n_row + row_at
    root_cols = lax.dynamic_slice_in_dim(linv_root, col_at * col_width, col_width, 1)
    term_value = contract_rows(linv_root, root_cols)
    column_panel = lax.psum(term_value, ("depth", "row"))
    sigma_root = lax.dynamic_slice_in_dim(column_panel, flat_at * root_rows, root_rows, 0)
    factor = child_factor[0]
    inverse = child_inverse[0]
    tile_mask = jnp.repeat(structure[0], TILE).astype(jnp.float32)[:, None]
    masked_factor = factor * tile_mask
    factor_panel = lax.all_gather(masked_factor, "row", axis=1, tiled=True)
    nj_row = factor.shape[1]
    inverse_block = lax.dynamic_slice_in_dim(inverse, row_at * nj_row, nj_row, 1)
    update = jnp.dot(
        factor_panel,
        lax.all_gather(inverse_block, "col", axis=0, tiled=True),
        precision=PRECISION,
        preferred_element_type=jnp.float32,
    )
    own_term, column_panel = lax.optimization_barrier((contract_rows(inverse, inverse_block), column_panel))
    weighted = contract_rows(column_panel, lax.all_gather(update, "col", axis=0, tiled=True))
    cross_block = -weighted * tile_mask
    update_panel = lax.all_gather(update, "row", axis=1, tiled=True)
    child_block = lax.psum_scatter(
        contract_rows(update_panel, weighted) + own_term,
        "col",
        scatter_dimension=0,
        tiled=True,
    )
    return (sigma_root, cross_block[None], child_block[None])


def solution(mesh):
    in_specs = (
        P(("depth", "row"), None),
        P("depth", "col", "row"),
        P("depth", "col", None),
        P("depth", "col"),
    )
    out_specs = (P(("depth", "row"), "col"), P("depth", "col", "row"), P("depth", "col", "row"))
    return jax.shard_map(shards, mesh=mesh, in_specs=in_specs, out_specs=out_specs, check_vma=False)
```

```python
import jax
import jax.numpy as jnp
from jax import lax
from jax.sharding import PartitionSpec as P

TILE = 128
PRECISION = lax.Precision.HIGH


def contract_rows(left, right):
    return lax.dot_general(
        left,
        right,
        (((0,), (0,)), ((), ())),
        precision=PRECISION,
        preferred_element_type=jnp.float32,
    )


def shards(linv_root, child_factor, child_inverse, structure):
    n_col = lax.axis_size("col")
    n_row = lax.axis_size("row")
    col_at = lax.axis_index("col")
    row_at = lax.axis_index("row")
    root_rows = linv_root.shape[0]
    col_width = linv_root.shape[1] // n_col
    flat_at = lax.axis_index("depth") * n_row + row_at
    root_cols = lax.dynamic_slice_in_dim(linv_root, col_at * col_width, col_width, 1)
    term_value = contract_rows(linv_root, root_cols)
    column_panel = lax.psum(term_value, ("depth", "row"))
    sigma_root = lax.dynamic_slice_in_dim(column_panel, flat_at * root_rows, root_rows, 0)
    factor = child_factor[0]
    inverse = child_inverse[0]
    tile_mask = jnp.repeat(structure[0], TILE).astype(jnp.float32)[:, None]
    factor_panel = lax.all_gather(factor, "row", axis=1, tiled=True)
    nj_row = factor.shape[1]
    inverse_block = lax.dynamic_slice_in_dim(inverse, row_at * nj_row, nj_row, 1)
    product = jnp.dot(
        factor_panel,
        lax.all_gather(inverse_block, "col", axis=0, tiled=True),
        precision=PRECISION,
        preferred_element_type=jnp.float32,
    )
    update = jnp.where(tile_mask > 0, product, 0.0)
    own_term, column_panel = lax.optimization_barrier((contract_rows(inverse, inverse_block), column_panel))
    weighted = contract_rows(column_panel, lax.all_gather(update, "col", axis=0, tiled=True))
    cross_block = -weighted * tile_mask
    update_panel = lax.all_gather(update, "row", axis=1, tiled=True)
    child_block = lax.psum_scatter(
        contract_rows(update_panel, weighted) + own_term,
        "col",
        scatter_dimension=0,
        tiled=True,
    )
    return (sigma_root, cross_block[None], child_block[None])


def solution(mesh):
    in_specs = (
        P(("depth", "row"), None),
        P("depth", "col", "row"),
        P("depth", "col", None),
        P("depth", "col"),
    )
    out_specs = (P(("depth", "row"), "col"), P("depth", "col", "row"), P("depth", "col", "row"))
    return jax.shard_map(shards, mesh=mesh, in_specs=in_specs, out_specs=out_specs, check_vma=False)
```
